512 devices in a mesh: ctx: 32 (over y, x), head: 16 (over z, core).
Axes of the slice: x: 4, y: 8, z: 8, core: 2. Of those that a mesh axis runs over, the one named last changes fastest.
Arguments:
- q_heads: bfloat16 [24576, 8192], P(('ctx', 'head')), may hold values from -16 to 16
- key_head_rows: bfloat16 [24576, 1024], P(('ctx', 'head')), may hold values from -30 to 30
- value_head_rows: bfloat16 [24576, 1024], P(('ctx', 'head')), may hold values from -6 to 6
- doc_lengths: int32 [16], replicated, may hold values from 1 to 3072, 24576 in all
Outputs:
- attended: bfloat16 [24576, 8192], P(('ctx', 'head'))
The draws below stay inside these ranges and needn't reach their ends.
Inputs may be any that keep to these rules, and one draw needn't show every extreme that they name: `doc_lengths`: they sum to 24576; the largest is exactly 3072.
All inputs are finite; a program needn't handle non-finite values. Where the reference program divides by a largest or mean magnitude, that divisor is 1e-20 or more.
Results may differ from the reference program's by a relative error of at most 0.018.
Values may be sent and summed in bfloat16 or wider, within the bound.
A program may use at most 128 MiB of HBM per device.

```python
import math
import jax
import jax.numpy as jnp
import numpy as np
from jax import lax

QUERY_HEADS = 64
KEY_HEADS = 8
HEAD_SIZE = 128
DOCS = 16
SLAB_TOKENS = 24576
MOST = 3072


def shared_base(key):
    return jnp.clip(jax.random.normal(key, (SLAB_TOKENS, KEY_HEADS, HEAD_SIZE), jnp.float32), -5.0, 5.0)


def position_ramp():
    return 1.0 + 2.0 * jnp.arange(SLAB_TOKENS, dtype=jnp.float32) / (SLAB_TOKENS - 1)


def draw_key_head_rows(key, part):
    base = shared_base(key)
    key = jax.random.fold_in(key, 1)
    key_gains = jnp.exp(jax.random.uniform(key, (KEY_HEADS,), jnp.float32, math.log(0.5), math.log(2.0)))
    key_rows = base * position_ramp()[:, None, None] * key_gains[None, :, None]
    return key_rows.reshape(SLAB_TOKENS, KEY_HEADS * HEAD_SIZE).astype(jnp.bfloat16)


def draw_q_heads(key, part):
    key = jax.random.fold_in(key, 2)
    noise = jax.random.normal(key, (SLAB_TOKENS, QUERY_HEADS, HEAD_SIZE), jnp.float32)
    return jnp.clip(noise, -16.0, 16.0).reshape(SLAB_TOKENS, QUERY_HEADS * HEAD_SIZE).astype(jnp.bfloat16)


def levels(rng, dims, shards, smallest, largest):
    def one(dim, parts):
        draws = jax.random.uniform(jax.random.fold_in(jax.random.fold_in(rng, 6), dim), (parts,), jnp.float32, smallest / len(shards), largest / len(shards))
        return jnp.repeat(jnp.exp(draws), dims[dim] // parts).reshape((-1,) + (1,) * (len(dims) - dim - 1))

    factor_of = one(*shards[0])
    for cut in shards[1:]:
        factor_of = factor_of * one(*cut)
    return factor_of


def profile(amount, total, bound, slope):
    weights = [(1 << 20) // math.isqrt(grade ** slope) + 1 for grade in range(2, amount + 1)]
    rest, given = total - bound - (amount - 1), [1] * (amount - 1)
    while rest > 0:
        movable = [i for i in range(amount - 1) if given[i] < bound]
        pool, left = sum([weights[i] for i in movable]), rest
        for i in movable:
            addition = min(bound - given[i], max(1, left * weights[i] // pool), rest)
            given[i] = given[i] + addition
            rest = rest - addition
    return np.array([bound] + given)


def uneven(own_key, amount, total, most, skew):
    if amount == 2:
        one = jax.random.randint(own_key, (), max(1, total - most), min(most, total - 1) + 1)
        return jnp.stack([one, total - one])
    sizes = jnp.asarray(profile(amount, total, most, skew), jnp.int32)
    twos = (amount - 1) // 2
    donor, sink = sizes[1:1 + 2 * twos:2], sizes[2:2 + 2 * twos:2]
    room = jnp.minimum(donor - 1, most - sink)
    moved = jax.random.randint(jax.random.fold_in(own_key, 1), (twos,), 0, 1 << 20) % (room + 1)
    sizes = sizes.at[1:1 + 2 * twos:2].set(donor - moved).at[2:2 + 2 * twos:2].set(sink + moved)
    return sizes[jax.random.permutation(jax.random.fold_in(own_key, 2), amount)]


def scatter_about(stream_key, shape, width, most, pieces=(), kind=jnp.bfloat16):
    values = jax.random.normal(stream_key, shape, jnp.float32) * width
    if len(pieces) > 0:
        values = levels(stream_key, shape, pieces, -0.22, 0.18) * values
    return jnp.clip(values, min=-most, max=most).astype(kind)


def setup_inputs(seed: int = 0) -> dict:
    streams_of = jax.random.split(jax.random.key(seed), 5)
    q_heads = draw_q_heads(jax.random.fold_in(streams_of[4], 71), 0)
    key_head_rows = draw_key_head_rows(jax.random.fold_in(streams_of[4], 71), 0)
    value_head_rows = scatter_about(streams_of[2], (SLAB_TOKENS, KEY_HEADS * HEAD_SIZE), 1.0, 6.0, ((0, 512),))
    doc_lengths = uneven(streams_of[3], DOCS, SLAB_TOKENS, MOST, 2).astype(jnp.int32)
    return dict(q_heads=q_heads, key_head_rows=key_head_rows, value_head_rows=value_head_rows, doc_lengths=doc_lengths)


KCLIP = 8.0
NEG = -1e+30

def doc_index(positions, doc_lengths):
    ends = jnp.cumsum(doc_lengths)
    return lax.optimization_barrier(jnp.sum((positions[:, None] >= ends[None, :]).astype(jnp.int32), axis=1))

def reference(q_heads, key_head_rows, value_head_rows, doc_lengths):
    positions = jnp.arange(SLAB_TOKENS, dtype=jnp.int32)
    docs = doc_index(positions, doc_lengths)
    key_float = key_head_rows.astype(jnp.float32).reshape(SLAB_TOKENS, KEY_HEADS, HEAD_SIZE)
    key_scale = lax.optimization_barrier(jnp.max(jnp.abs(key_float), axis=(0, 2)))
    key_rows = (key_float * (KCLIP / key_scale)[None, :, None]).astype(jnp.bfloat16)
    keys_t = jnp.transpose(key_rows, (1, 0, 2))
    value_columns = jnp.transpose(value_head_rows.reshape(SLAB_TOKENS, KEY_HEADS, HEAD_SIZE), (1, 0, 2))
    queries_t = jnp.transpose(q_heads.reshape(SLAB_TOKENS, QUERY_HEADS, HEAD_SIZE), (1, 0, 2))
    block = math.gcd(SLAB_TOKENS, 1024)
    blocks = SLAB_TOKENS // block
    group_size = QUERY_HEADS // KEY_HEADS
    inverse = 1.0 / math.sqrt(HEAD_SIZE)

    def one_head(args):
        q_head, index = args
        k_head = keys_t[index // group_size]
        v_head = value_columns[index // group_size]

        def one_block(block_args):
            q_blk, start = block_args
            q_pos = start + jnp.arange(block, dtype=jnp.int32)
            q_doc = lax.dynamic_slice_in_dim(docs, start, block)
            allowed = (positions[None, :] <= q_pos[:, None]) & (docs[None, :] == q_doc[:, None])
            scores = jnp.dot(q_blk, k_head.T, preferred_element_type=jnp.float32) * inverse
            scores = jnp.where(allowed, scores, NEG)
            top = lax.optimization_barrier(jnp.max(scores, axis=1, keepdims=True))
            expo = jnp.where(allowed, jnp.exp(scores - top), 0.0)
            total = lax.optimization_barrier(jnp.sum(expo, axis=1, keepdims=True))
            mixed = jnp.dot(expo.astype(jnp.bfloat16), v_head, preferred_element_type=jnp.float32)
            return (mixed / total).astype(jnp.bfloat16)
        starts = jnp.arange(blocks, dtype=jnp.int32) * block
        return lax.map(one_block, (q_head.reshape(blocks, block, HEAD_SIZE), starts)).reshape(SLAB_TOKENS, HEAD_SIZE)
    result = lax.map(one_head, (queries_t, jnp.arange(QUERY_HEADS, dtype=jnp.int32)))
    return jnp.transpose(result, (1, 0, 2)).reshape(SLAB_TOKENS, QUERY_HEADS * HEAD_SIZE)
```

```python
import math

import jax
import jax.numpy as jnp
from jax import lax
from jax.experimental import pallas as pl
from jax.experimental.pallas import tpu as pltpu
from jax.sharding import PartitionSpec as P

HEAD_SIZE = 128
KCLIP = 8.0
NEG = -1e30
MESH = pl.DeviceIdType.MESH
BF = jnp.bfloat16
F32 = jnp.float32
NX, NY, NZ = 4, 8, 8
SHARE = 48
CHIP = 2 * SHARE
BLOCK = NZ * CHIP
REACH = 4
OWN = REACH * NZ
KEYS = (REACH + 1) * BLOCK
GROUP = 4
COLS = GROUP * HEAD_SIZE
TILE = 192
TDEV = TILE // SHARE
TILES = BLOCK // TILE
ROWS = TILE * GROUP
CHUNKS = ((2304, 1024), (1536, 768), (768, 768), (0, 768))
DOCS = 16
NT = (((1,), (1,)), ((), ()))


def attend_tile(t, base, factor, ends, q_ref, k_ref, vt_ref, o_ref):
    start = pl.multiple_of((t * TILE) // 128 * 128, 128)
    rows = [q_ref[TDEV * t + d, :, HEAD_SIZE * j : HEAD_SIZE * (j + 1)] for j in range(GROUP) for d in range(TDEV)]
    queries = (jnp.concatenate(rows, axis=0).astype(F32) * factor).astype(BF)
    place = lax.rem(lax.broadcasted_iota(jnp.int32, (1, ROWS), 1), TILE)
    q_pos = base + t * TILE + place
    low = jnp.zeros((1, ROWS), jnp.int32)
    for e in ends:
        low = jnp.where(q_pos >= e, e, low)
    k_base = base - REACH * BLOCK + start
    low = low - k_base
    high = q_pos - k_base
    top = jnp.full((1, ROWS), NEG, F32)
    accum = jnp.zeros((HEAD_SIZE + 16, ROWS), F32)
    for first, size in CHUNKS:
        at = pl.multiple_of(start + first, 128)
        scores = lax.dot_general(k_ref[pl.ds(at, size), :], queries, NT, preferred_element_type=F32)
        k_row = lax.broadcasted_iota(jnp.int32, (size, ROWS), 0) + first
        allowed = k_row >= low
        if first + size > REACH * BLOCK:
            allowed = allowed & (k_row <= high)
        scores = jnp.where(allowed, scores, NEG)
        partial = jnp.max(scores.reshape(size // 8, 8, ROWS), axis=0)
        top_new = jnp.maximum(top, jnp.max(partial, axis=0, keepdims=True))
        expo = jnp.exp2(scores - top_new).astype(BF)
        contrib = jnp.dot(vt_ref[:, pl.ds(at, size)], expo, preferred_element_type=F32)
        accum = accum * jnp.exp2(top - top_new) + contrib
        top = top_new
    out = accum[:HEAD_SIZE] / accum[HEAD_SIZE : HEAD_SIZE + 1]
    out = out.T.astype(BF)
    for j in range(GROUP):
        for d in range(TDEV):
            r = (j * TDEV + d) * SHARE
            o_ref[TDEV * t + d, :, HEAD_SIZE * j : HEAD_SIZE * (j + 1)] = out[r : r + SHARE]


def kernel(
    len_ref, q_hbm, k_hbm, v_hbm, out_hbm,
    q_buf, o_buf, kv_buf, k_flat, vt, mine, tops_y, tops_x,
    q_send, q_recv, kv_send, kv_recv, y_send, y_recv, x_send, x_recv, d_send, d_recv,
    ty_send, ty_recv, tx_send, tx_recv, o_send, o_recv, local,
):
    c = lax.axis_index("ctx")
    h = lax.axis_index("head")
    x = lax.rem(c, NX)
    y = lax.div(c, NX)
    z = lax.div(h, 2)
    core = lax.rem(h, 2)
    heads = 2 * NZ

    def head_peer(k):
        return lax.rem(h + k, heads)

    def x_peer(k):
        return y * NX + lax.rem(x + k, NX)

    def y_peer(k):
        return lax.rem(y + k, NY) * NX + x

    sibling = h + 1 - 2 * core

    def remote(src, dst, send, recv, **where):
        return pltpu.make_async_remote_copy(
            src_ref=src, dst_ref=dst, send_sem=send, recv_sem=recv, device_id=where, device_id_type=MESH
        )

    barrier = pltpu.get_barrier_semaphore()
    for k in range(1, heads):
        pl.semaphore_signal(barrier, inc=1, device_id={"head": head_peer(k)}, device_id_type=MESH)
    for k in range(1, NX):
        pl.semaphore_signal(barrier, inc=1, device_id={"ctx": x_peer(k)}, device_id_type=MESH)
    for k in range(1, NY):
        pl.semaphore_signal(barrier, inc=1, device_id={"ctx": y_peer(k)}, device_id_type=MESH)
    pl.semaphore_wait(barrier, heads - 1 + NX - 1 + NY - 1)

    kv_copies = []
    for k in (1, 7, 2, 6, 3, 5, 4):
        other = lax.rem(z + k, NZ)
        lanes = pl.ds(pl.multiple_of(other * HEAD_SIZE, HEAD_SIZE), HEAD_SIZE)
        for i, source in enumerate((k_hbm, v_hbm)):
            copy = remote(
                source.at[:, lanes], kv_buf.at[i, OWN + z, core], kv_send.at[i, k], kv_recv.at[i, k], head=other * 2 + core
            )
            copy.start()
            kv_copies.append(copy)
    lanes = pl.ds(pl.multiple_of(z * HEAD_SIZE, HEAD_SIZE), HEAD_SIZE)
    kv_local = []
    for i, source in enumerate((k_hbm, v_hbm)):
        copy = pltpu.make_async_copy(source.at[:, lanes], kv_buf.at[i, OWN + z, core], local.at[i])
        copy.start()
        kv_local.append(copy)
    q_copies = []
    for k in (1, 15, 2, 14, 3, 13, 4, 12, 5, 11, 6, 10, 7, 9, 8):
        dest = head_peer(k)
        lanes = pl.ds(pl.multiple_of(dest * COLS, COLS), COLS)
        copy = remote(q_hbm.at[:, lanes], q_buf.at[h], q_send.at[k], q_recv.at[k], head=dest)
        copy.start()
        q_copies.append(copy)
    q_own = pltpu.make_async_copy(q_hbm.at[:, pl.ds(pl.multiple_of(h * COLS, COLS), COLS)], q_buf.at[h], local.at[2])
    q_own.start()

    ends = []
    total = jnp.int32(0)
    for i in range(DOCS):
        total = total + len_ref[i]
        ends.append(total)
    vt[HEAD_SIZE:, :] = jnp.ones((16, KEYS), BF)

    for copy in kv_local:
        copy.wait()
    for copy in kv_copies:
        copy.wait_recv()

    def half(i, slot):
        return kv_buf.at[i, pl.ds(slot, NZ), core]

    own_y, own_x, own_d = [], [], []
    for i in range(2):
        copy = remote(half(i, OWN), half(i, 0), y_send.at[i], y_recv.at[i], ctx=y_peer(1))
        copy.start()
        own_y.append(copy)

    def x_copy(i, k):
        slot = jnp.where(x + k < NX, OWN, 0)
        return remote(half(i, slot), half(i, OWN - k * NZ), x_send.at[i, k], x_recv.at[i, k], ctx=x_peer(k))

    for k in (1, 3, 2):
        @pl.when(x + k < NX)
        def _():
            for i in range(2):
                x_copy(i, k).start()

    def swap(i, b):
        return remote(half(i, b * NZ), half(i, b * NZ), d_send.at[i, b], d_recv.at[i, b], head=sibling)

    def flatten(b):
        k_flat[b * BLOCK : (b + 1) * BLOCK, :] = kv_buf[0, b * NZ : (b + 1) * NZ].reshape(BLOCK, HEAD_SIZE)
        values = kv_buf[1, b * NZ : (b + 1) * NZ].reshape(BLOCK, HEAD_SIZE)
        vt[:HEAD_SIZE, b * BLOCK : (b + 1) * BLOCK] = values.T

    for i in range(2):
        swap(i, REACH).start()
    for i in range(2):
        swap(i, REACH).wait_recv()

    magnitude = jnp.abs(kv_buf[0, OWN : OWN + NZ].reshape(BLOCK // 8, 8, HEAD_SIZE).astype(F32))
    mine[0] = jnp.max(magnitude, axis=0)
    y_tops = []
    for k in range(1, NY):
        copy = remote(mine.at[0], tops_y.at[k], ty_send.at[k], ty_recv.at[k], ctx=y_peer(k))
        copy.start()
        y_tops.append(copy)
    flatten(REACH)
    for copy in y_tops:
        copy.wait_recv()
    mine[1] = jnp.maximum(mine[0], jnp.max(tops_y[1:], axis=0))
    x_tops = []
    for k in range(1, NX):
        copy = remote(mine.at[1], tops_x.at[k], tx_send.at[k], tx_recv.at[k], ctx=x_peer(k))
        copy.start()
        x_tops.append(copy)

    for copy in own_y:
        copy.wait_recv()
    for k in (1, 3, 2):
        @pl.when(x + k >= NX)
        def _():
            for i in range(2):
                x_copy(i, k).start()
    for i in range(2):
        swap(i, 0).start()
    for copy in x_tops:
        copy.wait_recv()
    largest = jnp.max(jnp.maximum(mine[1], jnp.max(tops_x[1:], axis=0)))
    factor = jnp.full((1, HEAD_SIZE), KCLIP * math.log2(math.e) / math.sqrt(HEAD_SIZE), F32) / largest
    for i in range(2):
        swap(i, 0).wait_recv()
    flatten(0)
    for k in (1, 3, 2):
        for i in range(2):
            x_copy(i, k).wait_recv()
        for i in range(2):
            swap(i, REACH - k).start()
    for k in (1, 3, 2):
        for i in range(2):
            swap(i, REACH - k).wait_recv()
        flatten(REACH - k)
    q_own.wait()

    base = c * BLOCK
    own_tile = lax.div(z, 2)
    turn = 1 - 2 * lax.rem(own_tile, 2)

    def one_tile(s, carry):
        t = lax.rem(own_tile + turn * (s + 1) + TILES, TILES)
        for d in range(TDEV):
            dev = TDEV * t + d

            @pl.when(dev != h)
            def _():
                k = lax.rem(h - dev + heads, heads)
                remote(q_hbm.at[:, pl.ds(0, COLS)], q_buf.at[dev], q_send.at[k], q_recv.at[k], head=dev).wait_recv()

        attend_tile(t, base, factor, ends, q_buf, k_flat, vt, o_buf)
        lanes = pl.ds(pl.multiple_of(h * COLS, COLS), COLS)
        for d in range(TDEV):
            dev = TDEV * t + d

            @pl.when(dev != h)
            def _():
                remote(o_buf.at[dev], out_hbm.at[:, lanes], o_send.at[dev], o_recv.at[h], head=dev).start()

            @pl.when(dev == h)
            def _():
                pltpu.make_async_copy(o_buf.at[dev], out_hbm.at[:, lanes], local.at[3]).start()

        return carry

    lax.fori_loop(0, TILES, one_tile, 0)

    for copy in kv_copies + q_copies + own_y + y_tops + x_tops:
        copy.wait_send()
    for k in range(1, NX):
        for i in range(2):
            x_copy(i, k).wait_send()
    for b in range(REACH + 1):
        for i in range(2):
            swap(i, b).wait_send()
    pltpu.make_async_copy(o_buf.at[h], out_hbm.at[:, pl.ds(pl.multiple_of(h * COLS, COLS), COLS)], local.at[3]).wait()
    for k in range(1, heads):
        dev = head_peer(k)
        lanes = pl.ds(pl.multiple_of(dev * COLS, COLS), COLS)
        remote(o_buf.at[dev], out_hbm.at[:, lanes], o_send.at[dev], o_recv.at[dev], head=dev).wait()


def on_device(q, k, v, doc_lengths):
    any_space = pl.BlockSpec(memory_space=pl.ANY)
    dma = pltpu.SemaphoreType.DMA
    return pl.pallas_call(
        kernel,
        out_shape=jax.ShapeDtypeStruct(q.shape, BF),
        in_specs=[pl.BlockSpec(memory_space=pltpu.SMEM), any_space, any_space, any_space],
        out_specs=any_space,
        scratch_shapes=[
            pltpu.VMEM((2 * NZ, SHARE, COLS), BF),
            pltpu.VMEM((2 * NZ, SHARE, COLS), BF),
            pltpu.VMEM((2, OWN + NZ, 2, SHARE, HEAD_SIZE), BF),
            pltpu.VMEM((KEYS, HEAD_SIZE), BF),
            pltpu.VMEM((HEAD_SIZE + 16, KEYS), BF),
            pltpu.VMEM((2, 8, HEAD_SIZE), F32),
            pltpu.VMEM((NY, 8, HEAD_SIZE), F32),
            pltpu.VMEM((NX, 8, HEAD_SIZE), F32),
            dma((2 * NZ,)), dma((2 * NZ,)),
            dma((2, NZ)), dma((2, NZ)),
            dma((2,)), dma((2,)),
            dma((2, NX)), dma((2, NX)),
            dma((2, REACH + 1)), dma((2, REACH + 1)),
            dma((NY,)), dma((NY,)),
            dma((NX,)), dma((NX,)),
            dma((2 * NZ,)), dma((2 * NZ,)),
            dma((4,)),
        ],
        compiler_params=pltpu.CompilerParams(collective_id=0, has_side_effects=True, vmem_limit_bytes=56 << 20),
        cost_estimate=pl.CostEstimate(flops=5_200_000_000, bytes_accessed=2_000_000, transcendentals=10_000_000),
    )(doc_lengths, q, k, v)


def solution(mesh):
    rows = P(("ctx", "head"), None)
    return jax.shard_map(on_device, mesh=mesh, in_specs=(rows, rows, rows, P()), out_specs=rows, check_vma=False)
```

```python
import math

import jax
import jax.numpy as jnp
from jax import lax
from jax.experimental import pallas as pl
from jax.experimental.pallas import tpu as pltpu
from jax.sharding import PartitionSpec as P

HEAD_SIZE = 128
KCLIP = 8.0
NEG = -1e30
MESH = pl.DeviceIdType.MESH
BF = jnp.bfloat16
F32 = jnp.float32
NX, NY, NZ = 4, 8, 8
SHARE = 48
CHIP = 2 * SHARE
BLOCK = NZ * CHIP
REACH = 4
OWN = REACH * NZ
KEYS = (REACH + 1) * BLOCK
GROUP = 4
COLS = GROUP * HEAD_SIZE
TILE = 192
TDEV = TILE // SHARE
TILES = BLOCK // TILE
ROWS = TILE * GROUP
WINDOW = 3328
CHUNK = 256
DOCS = 16
NT = (((1,), (1,)), ((), ()))


class Tile:
    def __init__(self, t, start, base, factor, ends, q_ref):
        rows = [q_ref[TDEV * t + d, :, HEAD_SIZE * j : HEAD_SIZE * (j + 1)] for j in range(GROUP) for d in range(TDEV)]
        self.queries = (jnp.concatenate(rows, axis=0).astype(F32) * factor).astype(BF)
        place = lax.rem(lax.broadcasted_iota(jnp.int32, (1, ROWS), 1), TILE)
        q_pos = base + t * TILE + place
        low = jnp.zeros((1, ROWS), jnp.int32)
        for e in ends:
            low = jnp.where(q_pos >= e, e, low)
        k_base = base - REACH * BLOCK + start
        self.low, self.high = low - k_base, q_pos - k_base
        self.start = start
        self.top = jnp.full((1, ROWS), NEG, F32)
        self.accum = jnp.zeros((HEAD_SIZE + 16, ROWS), F32)

    def scores(self, first, k_ref):
        at = pl.ds(pl.multiple_of(self.start + first, 128), CHUNK)
        scores = lax.dot_general(k_ref[at, :], self.queries, NT, preferred_element_type=F32)
        k_row = lax.broadcasted_iota(jnp.int32, (CHUNK, ROWS), 0) + first
        allowed = k_row >= self.low
        if first + CHUNK > REACH * BLOCK:
            allowed = allowed & (k_row <= self.high)
        return jnp.where(allowed, scores, NEG)

    def visit(self, firsts, k_ref, vt_ref):
        coming = self.scores(firsts[0], k_ref)
        for n, first in enumerate(firsts):
            scores = coming
            partial = jnp.max(scores.reshape(CHUNK // 8, 8, ROWS), axis=0)
            top = jnp.maximum(self.top, jnp.max(partial, axis=0, keepdims=True))
            if n + 1 < len(firsts):
                coming = self.scores(firsts[n + 1], k_ref)
            expo = jnp.exp2(scores - top).astype(BF)
            at = pl.ds(pl.multiple_of(self.start + first, 128), CHUNK)
            contrib = jnp.dot(vt_ref[:, at], expo, preferred_element_type=F32)
            self.accum = self.accum * jnp.exp2(self.top - top) + contrib
            self.top = top

    def store(self, t, o_ref):
        out = self.accum[:HEAD_SIZE] / self.accum[HEAD_SIZE : HEAD_SIZE + 1]
        out = out.T.astype(BF)
        for j in range(GROUP):
            for d in range(TDEV):
                r = (j * TDEV + d) * SHARE
                o_ref[TDEV * t + d, :, HEAD_SIZE * j : HEAD_SIZE * (j + 1)] = out[r : r + SHARE]


def kernel(
    len_ref, q_hbm, k_hbm, v_hbm, out_hbm,
    q_buf, o_buf, kv_buf, k_flat, vt, mine, tops_y, tops_x,
    q_send, q_recv, kv_send, kv_recv, y_send, y_recv, x_send, x_recv, d_send, d_recv,
    ty_send, ty_recv, tx_send, tx_recv, o_send, o_recv, local,
):
    c = lax.axis_index("ctx")
    h = lax.axis_index("head")
    x = lax.rem(c, NX)
    y = lax.div(c, NX)
    z = lax.div(h, 2)
    core = lax.rem(h, 2)
    heads = 2 * NZ

    def head_peer(k):
        return lax.rem(h + k, heads)

    def x_peer(k):
        return y * NX + lax.rem(x + k, NX)

    def y_peer(k):
        return lax.rem(y + k, NY) * NX + x

    sibling = h + 1 - 2 * core

    def remote(src, dst, send, recv, **where):
        return pltpu.make_async_remote_copy(
            src_ref=src, dst_ref=dst, send_sem=send, recv_sem=recv, device_id=where, device_id_type=MESH
        )

    barrier = pltpu.get_barrier_semaphore()
    for k in range(1, heads):
        pl.semaphore_signal(barrier, inc=1, device_id={"head": head_peer(k)}, device_id_type=MESH)
    for k in range(1, NX):
        pl.semaphore_signal(barrier, inc=1, device_id={"ctx": x_peer(k)}, device_id_type=MESH)
        pl.semaphore_signal(barrier, inc=1, device_id={"ctx": x_peer(k), "head": sibling}, device_id_type=MESH)
    for k in range(1, NY):
        pl.semaphore_signal(barrier, inc=1, device_id={"ctx": y_peer(k)}, device_id_type=MESH)
    pl.semaphore_wait(barrier, heads - 1 + 2 * (NX - 1) + NY - 1)

    kv_copies = ([], [])
    for i, source in enumerate((k_hbm, v_hbm)):
        for k in (4, 3, 5, 2, 6, 1, 7):
            other = lax.rem(z + k, NZ)
            lanes = pl.ds(pl.multiple_of(other * HEAD_SIZE, HEAD_SIZE), HEAD_SIZE)
            copy = remote(
                source.at[:, lanes], kv_buf.at[i, OWN + z, core], kv_send.at[i, k], kv_recv.at[i, k], head=other * 2 + core
            )
            copy.start()
            kv_copies[i].append(copy)
    lanes = pl.ds(pl.multiple_of(z * HEAD_SIZE, HEAD_SIZE), HEAD_SIZE)
    kv_local = []
    for i, source in enumerate((k_hbm, v_hbm)):
        copy = pltpu.make_async_copy(source.at[:, lanes], kv_buf.at[i, OWN + z, core], local.at[i])
        copy.start()
        kv_local.append(copy)
    q_copies = []
    for k in (1, 15, 2, 14, 3, 13, 4, 12, 5, 11, 6, 10, 7, 9, 8):
        dest = head_peer(k)
        lanes = pl.ds(pl.multiple_of(dest * COLS, COLS), COLS)
        copy = remote(q_hbm.at[:, lanes], q_buf.at[h], q_send.at[k], q_recv.at[k], head=dest)
        copy.start()
        q_copies.append(copy)
    q_own = pltpu.make_async_copy(q_hbm.at[:, pl.ds(pl.multiple_of(h * COLS, COLS), COLS)], q_buf.at[h], local.at[2])
    q_own.start()

    ends = []
    total = jnp.int32(0)
    for i in range(DOCS):
        total = total + len_ref[i]
        ends.append(total)
    vt[HEAD_SIZE:, :] = jnp.ones((16, KEYS), BF)

    def half(i, slot):
        return kv_buf.at[i, pl.ds(slot, NZ), core]

    def y_copy(i):
        return remote(half(i, OWN), half(i, 0), y_send.at[i], y_recv.at[i], ctx=y_peer(1))

    def x_copy(i, k):
        slot = jnp.where(x + k < NX, OWN, 0)
        return remote(half(i, slot), half(i, OWN - k * NZ), x_send.at[i, k], x_recv.at[i, k], ctx=x_peer(k))

    def swap(i, b):
        return remote(half(i, b * NZ), half(i, b * NZ), d_send.at[i, b], d_recv.at[i, b], head=sibling)

    def flatten(b):
        for i in range(2):
            swap(i, b).wait_recv()
        k_flat[b * BLOCK : (b + 1) * BLOCK, :] = kv_buf[0, b * NZ : (b + 1) * NZ].reshape(BLOCK, HEAD_SIZE)
        values = kv_buf[1, b * NZ : (b + 1) * NZ].reshape(BLOCK, HEAD_SIZE)
        vt[:HEAD_SIZE, b * BLOCK : (b + 1) * BLOCK] = values.T

    y_tops, x_tops = [], []
    for i in range(2):
        kv_local[i].wait()
        for copy in kv_copies[i]:
            copy.wait_recv()
        y_copy(i).start()
        for k in (1, 3, 2):
            @pl.when(x + k < NX)
            def _():
                x_copy(i, k).start()
        swap(i, REACH).start()
        if i == 0:
            keys = kv_buf[0, pl.ds(OWN, NZ), core].reshape(NZ * SHARE // 8, 8, HEAD_SIZE)
            mine[0] = jnp.max(jnp.abs(keys.astype(F32)), axis=0)
            for k in range(1, NY):
                copy = remote(mine.at[0], tops_y.at[k], ty_send.at[k], ty_recv.at[k], ctx=y_peer(k))
                copy.start()
                y_tops.append(copy)
    for i in range(2):
        y_copy(i).wait_recv()
        for k in (1, 3, 2):
            @pl.when(x + k >= NX)
            def _():
                x_copy(i, k).start()
        swap(i, 0).start()
        if i == 0:
            for copy in y_tops:
                copy.wait_recv()
            mine[1] = jnp.maximum(mine[0], jnp.max(tops_y[1:], axis=0))
            for k in range(NX):
                for far in (0, 1):
                    if k + far > 0:
                        there = {"ctx": x_peer(k), "head": sibling if far else h}
                        copy = remote(mine.at[1], tops_x.at[k, far], tx_send.at[k, far], tx_recv.at[k, far], **there)
                        copy.start()
                        x_tops.append(copy)
    flatten(REACH)
    for copy in x_tops:
        copy.wait_recv()
    tops_x[0, 0] = mine[1]
    largest = jnp.max(tops_x[...])
    factor = jnp.full((1, HEAD_SIZE), KCLIP * math.log2(math.e) / math.sqrt(HEAD_SIZE), F32) / largest
    q_own.wait()

    base = c * BLOCK
    own_tile = lax.div(z, 2)
    turn = 1 - 2 * lax.rem(z, 2)

    def tile_at(s):
        return lax.rem(own_tile + turn * (s + 1) + TILES, TILES)

    def await_queries(t):
        for d in range(TDEV):
            dev = TDEV * t + d

            @pl.when(dev != h)
            def _():
                k = lax.rem(h - dev + heads, heads)
                remote(q_hbm.at[:, pl.ds(0, COLS)], q_buf.at[dev], q_send.at[k], q_recv.at[k], head=dev).wait_recv()

    def send_out(t):
        lanes = pl.ds(pl.multiple_of(h * COLS, COLS), COLS)
        for d in range(TDEV):
            dev = TDEV * t + d

            @pl.when(dev != h)
            def _():
                remote(o_buf.at[dev], out_hbm.at[:, lanes], o_send.at[dev], o_recv.at[h], head=dev).start()

            @pl.when(dev == h)
            def _():
                pltpu.make_async_copy(o_buf.at[dev], out_hbm.at[:, lanes], local.at[3]).start()

    t = tile_at(0)
    await_queries(t)
    tile = Tile(t, 0, base, factor, ends, q_buf)
    block = [b * BLOCK + n * CHUNK for b in range(REACH + 1) for n in range(BLOCK // CHUNK)]
    parts = BLOCK // CHUNK
    tile.visit(block[REACH * parts :], k_flat, vt)
    flatten(0)
    tile.visit(block[:parts], k_flat, vt)
    for k in (1, 3, 2):
        for i in range(2):
            x_copy(i, k).wait_recv()
            swap(i, REACH - k).start()
    for k in (1, 3, 2):
        b = REACH - k
        flatten(b)
        tile.visit(block[b * parts : (b + 1) * parts], k_flat, vt)
    tile.store(t, o_buf)
    send_out(t)

    def one_tile(s, carry):
        t = tile_at(s)
        await_queries(t)
        tile = Tile(t, pl.multiple_of((t * TILE) // 128 * 128, 128), base, factor, ends, q_buf)
        tile.visit(list(reversed(range(0, WINDOW, CHUNK))), k_flat, vt)
        tile.store(t, o_buf)
        send_out(t)
        return carry

    lax.fori_loop(1, TILES, one_tile, 0)

    for copy in kv_copies[0] + kv_copies[1] + q_copies + y_tops + x_tops:
        copy.wait_send()
    for i in range(2):
        y_copy(i).wait_send()
    for k in range(1, NX):
        for i in range(2):
            x_copy(i, k).wait_send()
    for b in range(REACH + 1):
        for i in range(2):
            swap(i, b).wait_send()
    pltpu.make_async_copy(o_buf.at[h], out_hbm.at[:, pl.ds(pl.multiple_of(h * COLS, COLS), COLS)], local.at[3]).wait()
    for k in range(1, heads):
        dev = head_peer(k)
        lanes = pl.ds(pl.multiple_of(dev * COLS, COLS), COLS)
        remote(o_buf.at[dev], out_hbm.at[:, lanes], o_send.at[dev], o_recv.at[dev], head=dev).wait()


def on_device(q, k, v, doc_lengths):
    any_space = pl.BlockSpec(memory_space=pl.ANY)
    dma = pltpu.SemaphoreType.DMA
    return pl.pallas_call(
        kernel,
        out_shape=jax.ShapeDtypeStruct(q.shape, BF),
        in_specs=[pl.BlockSpec(memory_space=pltpu.SMEM), any_space, any_space, any_space],
        out_specs=any_space,
        scratch_shapes=[
            pltpu.VMEM((2 * NZ, SHARE, COLS), BF),
            pltpu.VMEM((2 * NZ, SHARE, COLS), BF),
            pltpu.VMEM((2, OWN + NZ, 2, SHARE, HEAD_SIZE), BF),
            pltpu.VMEM((KEYS, HEAD_SIZE), BF),
            pltpu.VMEM((HEAD_SIZE + 16, KEYS), BF),
            pltpu.VMEM((2, 8, HEAD_SIZE), F32),
            pltpu.VMEM((NY, 8, HEAD_SIZE), F32),
            pltpu.VMEM((NX, 2, 8, HEAD_SIZE), F32),
            dma((2 * NZ,)), dma((2 * NZ,)),
            dma((2, NZ)), dma((2, NZ)),
            dma((2,)), dma((2,)),
            dma((2, NX)), dma((2, NX)),
            dma((2, REACH + 1)), dma((2, REACH + 1)),
            dma((NY,)), dma((NY,)),
            dma((NX, 2)), dma((NX, 2)),
            dma((2 * NZ,)), dma((2 * NZ,)),
            dma((4,)),
        ],
        compiler_params=pltpu.CompilerParams(collective_id=0, has_side_effects=True, vmem_limit_bytes=56 << 20),
        cost_estimate=pl.CostEstimate(flops=5_200_000_000, bytes_accessed=2_000_000, transcendentals=10_000_000),
    )(doc_lengths, q, k, v)


def solution(mesh):
    rows = P(("ctx", "head"), None)
    return jax.shard_map(on_device, mesh=mesh, in_specs=(rows, rows, rows, P()), out_specs=rows, check_vma=False)
```

```python
import math

import jax
import jax.numpy as jnp
from jax import lax
from jax.experimental import pallas as pl
from jax.experimental.pallas import tpu as pltpu
from jax.sharding import PartitionSpec as P

HEAD_SIZE = 128
KCLIP = 8.0
NEG = -1e30
MESH = pl.DeviceIdType.MESH
BF = jnp.bfloat16
F32 = jnp.float32
NX, NY, NZ = 4, 8, 8
SHARE = 48
CHIP = 2 * SHARE
BLOCK = NZ * CHIP
REACH = 4
OWN = REACH * NZ
KEYS = (REACH + 1) * BLOCK
GROUP = 4
COLS = GROUP * HEAD_SIZE
TILE = 192
TDEV = TILE // SHARE
TILES = BLOCK // TILE
ROWS = TILE * GROUP
WINDOW = 3328
CHUNK = 256
DOCS = 16
NT = (((1,), (1,)), ((), ()))


class Tile:
    def __init__(self, t, start, base, factor, ends, q_ref):
        rows = [q_ref[TDEV * t + d, :, HEAD_SIZE * j : HEAD_SIZE * (j + 1)] for j in range(GROUP) for d in range(TDEV)]
        self.queries = (jnp.concatenate(rows, axis=0).astype(F32) * factor).astype(BF)
        place = lax.rem(lax.broadcasted_iota(jnp.int32, (1, ROWS), 1), TILE)
        q_pos = base + t * TILE + place
        low = jnp.zeros((1, ROWS), jnp.int32)
        for e in ends:
            low = jnp.where(q_pos >= e, e, low)
        k_base = base - REACH * BLOCK + start
        self.low, self.high = low - k_base, q_pos - k_base
        self.start = start
        self.top = jnp.full((1, ROWS), NEG, F32)
        self.accum = jnp.zeros((HEAD_SIZE + 16, ROWS), F32)

    def scores(self, first, k_ref):
        at = pl.ds(pl.multiple_of(self.start + first, 128), CHUNK)
        scores = lax.dot_general(k_ref[at, :], self.queries, NT, preferred_element_type=F32)
        k_row = lax.broadcasted_iota(jnp.int32, (CHUNK, ROWS), 0) + first
        allowed = k_row >= self.low
        if first + CHUNK > REACH * BLOCK:
            allowed = allowed & (k_row <= self.high)
        return jnp.where(allowed, scores, NEG)

    def visit(self, firsts, k_ref, vt_ref):
        coming = self.scores(firsts[0], k_ref)
        for n, first in enumerate(firsts):
            scores = coming
            partial = jnp.max(scores.reshape(CHUNK // 8, 8, ROWS), axis=0)
            top = jnp.maximum(self.top, jnp.max(partial, axis=0, keepdims=True))
            if n + 1 < len(firsts):
                coming = self.scores(firsts[n + 1], k_ref)
            expo = jnp.exp2(scores - top).astype(BF)
            at = pl.ds(pl.multiple_of(self.start + first, 128), CHUNK)
            contrib = jnp.dot(vt_ref[:, at], expo, preferred_element_type=F32)
            self.accum = self.accum * jnp.exp2(self.top - top) + contrib
            self.top = top

    def store(self, t, o_ref):
        out = self.accum[:HEAD_SIZE] * (1.0 / self.accum[HEAD_SIZE : HEAD_SIZE + 1])
        out = out.T.astype(BF)
        for j in range(GROUP):
            for d in range(TDEV):
                r = (j * TDEV + d) * SHARE
                o_ref[TDEV * t + d, :, HEAD_SIZE * j : HEAD_SIZE * (j + 1)] = out[r : r + SHARE]


def kernel(
    len_ref, q_hbm, k_hbm, v_hbm, out_hbm,
    q_buf, o_buf, kv_buf, k_flat, vt, mine, tops_y, tops_x,
    q_send, q_recv, kv_send, kv_recv, y_send, y_recv, x_send, x_recv, d_send, d_recv,
    ty_send, ty_recv, tx_send, tx_recv, o_send, o_recv, local,
):
    c = lax.axis_index("ctx")
    h = lax.axis_index("head")
    x = lax.rem(c, NX)
    y = lax.div(c, NX)
    z = lax.div(h, 2)
    core = lax.rem(h, 2)
    heads = 2 * NZ

    def head_peer(k):
        return lax.rem(h + k, heads)

    def x_peer(k):
        return y * NX + lax.rem(x + k, NX)

    def y_peer(k):
        return lax.rem(y + k, NY) * NX + x

    sibling = h + 1 - 2 * core

    def remote(src, dst, send, recv, **where):
        return pltpu.make_async_remote_copy(
            src_ref=src, dst_ref=dst, send_sem=send, recv_sem=recv, device_id=where, device_id_type=MESH
        )

    barrier = pltpu.get_barrier_semaphore()
    for k in range(1, heads):
        pl.semaphore_signal(barrier, inc=1, device_id={"head": head_peer(k)}, device_id_type=MESH)
    for k in range(1, NX):
        pl.semaphore_signal(barrier, inc=1, device_id={"ctx": x_peer(k)}, device_id_type=MESH)
        pl.semaphore_signal(barrier, inc=1, device_id={"ctx": x_peer(k), "head": sibling}, device_id_type=MESH)
    for k in range(1, NY):
        pl.semaphore_signal(barrier, inc=1, device_id={"ctx": y_peer(k)}, device_id_type=MESH)
    pl.semaphore_wait(barrier, heads - 1 + 2 * (NX - 1) + NY - 1)

    kv_copies = ([], [])
    for i, source in enumerate((k_hbm, v_hbm)):
        for k in (4, 3, 5, 2, 6, 1, 7):
            other = lax.rem(z + k, NZ)
            lanes = pl.ds(pl.multiple_of(other * HEAD_SIZE, HEAD_SIZE), HEAD_SIZE)
            copy = remote(
                source.at[:, lanes], kv_buf.at[i, OWN + z, core], kv_send.at[i, k], kv_recv.at[i, k], head=other * 2 + core
            )
            copy.start()
            kv_copies[i].append(copy)
    lanes = pl.ds(pl.multiple_of(z * HEAD_SIZE, HEAD_SIZE), HEAD_SIZE)
    kv_local = []
    for i, source in enumerate((k_hbm, v_hbm)):
        copy = pltpu.make_async_copy(source.at[:, lanes], kv_buf.at[i, OWN + z, core], local.at[i])
        copy.start()
        kv_local.append(copy)
    q_copies = []
    for k in (1, 15, 2, 14, 3, 13, 4, 12, 5, 11, 6, 10, 7, 9, 8):
        dest = head_peer(k)
        lanes = pl.ds(pl.multiple_of(dest * COLS, COLS), COLS)
        copy = remote(q_hbm.at[:, lanes], q_buf.at[h], q_send.at[k], q_recv.at[k], head=dest)
        copy.start()
        q_copies.append(copy)
    q_own = pltpu.make_async_copy(q_hbm.at[:, pl.ds(pl.multiple_of(h * COLS, COLS), COLS)], q_buf.at[h], local.at[2])
    q_own.start()

    ends = []
    total = jnp.int32(0)
    for i in range(DOCS):
        total = total + len_ref[i]
        ends.append(total)
    vt[HEAD_SIZE:, :] = jnp.ones((16, KEYS), BF)

    def half(i, slot):
        return kv_buf.at[i, pl.ds(slot, NZ), core]

    def y_copy(i):
        return remote(half(i, OWN), half(i, 0), y_send.at[i], y_recv.at[i], ctx=y_peer(1))

    def x_copy(i, k):
        slot = jnp.where(x + k < NX, OWN, 0)
        return remote(half(i, slot), half(i, OWN - k * NZ), x_send.at[i, k], x_recv.at[i, k], ctx=x_peer(k))

    def swap(i, b):
        return remote(half(i, b * NZ), half(i, b * NZ), d_send.at[i, b], d_recv.at[i, b], head=sibling)

    def flatten(b):
        for i in range(2):
            swap(i, b).wait_recv()
        k_flat[b * BLOCK : (b + 1) * BLOCK, :] = kv_buf[0, b * NZ : (b + 1) * NZ].reshape(BLOCK, HEAD_SIZE)
        values = kv_buf[1, b * NZ : (b + 1) * NZ].reshape(BLOCK, HEAD_SIZE)
        vt[:HEAD_SIZE, b * BLOCK : (b + 1) * BLOCK] = values.T

    y_tops, x_tops = [], []
    for i in range(2):
        kv_local[i].wait()
        for copy in kv_copies[i]:
            copy.wait_recv()
        y_copy(i).start()
        for k in (1, 3, 2):
            @pl.when(x + k < NX)
            def _():
                x_copy(i, k).start()
        swap(i, REACH).start()
        if i == 0:
            keys = kv_buf[0, pl.ds(OWN, NZ), core].reshape(NZ * SHARE // 8, 8, HEAD_SIZE)
            mine[0] = jnp.max(jnp.abs(keys.astype(F32)), axis=0)
            for k in range(1, NY):
                copy = remote(mine.at[0], tops_y.at[k], ty_send.at[k], ty_recv.at[k], ctx=y_peer(k))
                copy.start()
                y_tops.append(copy)
    for i in range(2):
        y_copy(i).wait_recv()
        for k in (1, 3, 2):
            @pl.when(x + k >= NX)
            def _():
                x_copy(i, k).start()
        swap(i, 0).start()
        if i == 0:
            for copy in y_tops:
                copy.wait_recv()
            mine[1] = jnp.maximum(mine[0], jnp.max(tops_y[1:], axis=0))
            for k in range(NX):
                for far in (0, 1):
                    if k + far > 0:
                        there = {"ctx": x_peer(k), "head": sibling if far else h}
                        copy = remote(mine.at[1], tops_x.at[k, far], tx_send.at[k, far], tx_recv.at[k, far], **there)
                        copy.start()
                        x_tops.append(copy)
    flatten(REACH)
    for copy in x_tops:
        copy.wait_recv()
    tops_x[0, 0] = mine[1]
    largest = jnp.max(tops_x[...])
    factor = jnp.full((1, HEAD_SIZE), KCLIP * math.log2(math.e) / math.sqrt(HEAD_SIZE), F32) / largest
    q_own.wait()

    base = c * BLOCK
    own_tile = lax.div(z, 2)
    turn = 1 - 2 * lax.rem(z, 2)

    def tile_at(s):
        return lax.rem(own_tile + turn * (s + 1) + TILES, TILES)

    def await_queries(t):
        for d in range(TDEV):
            dev = TDEV * t + d

            @pl.when(dev != h)
            def _():
                k = lax.rem(h - dev + heads, heads)
                remote(q_hbm.at[:, pl.ds(0, COLS)], q_buf.at[dev], q_send.at[k], q_recv.at[k], head=dev).wait_recv()

    def send_out(t):
        lanes = pl.ds(pl.multiple_of(h * COLS, COLS), COLS)
        for d in range(TDEV):
            dev = TDEV * t + d

            @pl.when(dev != h)
            def _():
                remote(o_buf.at[dev], out_hbm.at[:, lanes], o_send.at[dev], o_recv.at[h], head=dev).start()

            @pl.when(dev == h)
            def _():
                pltpu.make_async_copy(o_buf.at[dev], out_hbm.at[:, lanes], local.at[3]).start()

    t = tile_at(0)
    await_queries(t)
    tile = Tile(t, 0, base, factor, ends, q_buf)
    block = [b * BLOCK + n * CHUNK for b in range(REACH + 1) for n in range(BLOCK // CHUNK)]
    parts = BLOCK // CHUNK
    tile.visit(block[REACH * parts :], k_flat, vt)
    flatten(0)
    tile.visit(block[:parts], k_flat, vt)
    for near in ((1, 3), (2,)):
        for k in near:
            for i in range(2):
                x_copy(i, k).wait_recv()
                swap(i, REACH - k).start()
        for k in near:
            b = REACH - k
            flatten(b)
            tile.visit(block[b * parts : (b + 1) * parts], k_flat, vt)
    tile.store(t, o_buf)
    send_out(t)

    def one_tile(s, carry):
        t = tile_at(s)
        await_queries(t)
        tile = Tile(t, pl.multiple_of((t * TILE) // 128 * 128, 128), base, factor, ends, q_buf)
        tile.visit(list(reversed(range(0, WINDOW, CHUNK))), k_flat, vt)
        tile.store(t, o_buf)
        send_out(t)
        return carry

    lax.fori_loop(1, TILES, one_tile, 0)

    for copy in kv_copies[0] + kv_copies[1] + q_copies + y_tops + x_tops:
        copy.wait_send()
    for i in range(2):
        y_copy(i).wait_send()
    for k in range(1, NX):
        for i in range(2):
            x_copy(i, k).wait_send()
    for b in range(REACH + 1):
        for i in range(2):
            swap(i, b).wait_send()
    pltpu.make_async_copy(o_buf.at[h], out_hbm.at[:, pl.ds(pl.multiple_of(h * COLS, COLS), COLS)], local.at[3]).wait()
    for k in range(1, heads):
        dev = head_peer(k)
        lanes = pl.ds(pl.multiple_of(dev * COLS, COLS), COLS)
        remote(o_buf.at[dev], out_hbm.at[:, lanes], o_send.at[dev], o_recv.at[dev], head=dev).wait()


def on_device(q, k, v, doc_lengths):
    any_space = pl.BlockSpec(memory_space=pl.ANY)
    dma = pltpu.SemaphoreType.DMA
    return pl.pallas_call(
        kernel,
        out_shape=jax.ShapeDtypeStruct(q.shape, BF),
        in_specs=[pl.BlockSpec(memory_space=pltpu.SMEM), any_space, any_space, any_space],
        out_specs=any_space,
        scratch_shapes=[
            pltpu.VMEM((2 * NZ, SHARE, COLS), BF),
            pltpu.VMEM((2 * NZ, SHARE, COLS), BF),
            pltpu.VMEM((2, OWN + NZ, 2, SHARE, HEAD_SIZE), BF),
            pltpu.VMEM((KEYS, HEAD_SIZE), BF),
            pltpu.VMEM((HEAD_SIZE + 16, KEYS), BF),
            pltpu.VMEM((2, 8, HEAD_SIZE), F32),
            pltpu.VMEM((NY, 8, HEAD_SIZE), F32),
            pltpu.VMEM((NX, 2, 8, HEAD_SIZE), F32),
            dma((2 * NZ,)), dma((2 * NZ,)),
            dma((2, NZ)), dma((2, NZ)),
            dma((2,)), dma((2,)),
            dma((2, NX)), dma((2, NX)),
            dma((2, REACH + 1)), dma((2, REACH + 1)),
            dma((NY,)), dma((NY,)),
            dma((NX, 2)), dma((NX, 2)),
            dma((2 * NZ,)), dma((2 * NZ,)),
            dma((4,)),
        ],
        compiler_params=pltpu.CompilerParams(collective_id=0, has_side_effects=True, vmem_limit_bytes=56 << 20),
        cost_estimate=pl.CostEstimate(flops=5_200_000_000, bytes_accessed=2_000_000, transcendentals=10_000_000),
    )(doc_lengths, q, k, v)


def solution(mesh):
    rows = P(("ctx", "head"), None)
    return jax.shard_map(on_device, mesh=mesh, in_specs=(rows, rows, rows, P()), out_specs=rows, check_vma=False)
```
